256 devices in a mesh: seq: 16 (over x_lo, y, core), fsdp: 16 (over x_hi, z).
Axes of the slice: x: 4 (x_hi: 2, x_lo: 2; x = x_hi * 2 + x_lo), y: 4, z: 8, core: 2. Of those that a mesh axis runs over, the one named last changes fastest.
Arguments:
- tokens: bfloat16 [16, 2048, 4096], P('fsdp', 'seq'), may hold values from -6 to 6
- w_query: float32 [4096, 4096], P('fsdp', 'seq'), may hold values from -0.09375 to 0.09375
- w_key: float32 [4096, 4096], P('fsdp', 'seq'), may hold values from -0.09375 to 0.09375
- w_value: float32 [4096, 4096], P('fsdp', 'seq'), may hold values from -0.09375 to 0.09375
- short_taps: float32 [3, 3, 4096], P(None, None, 'seq'), may hold values from -4 to 4
- residue: float32 [4096, 16], P('seq'), may hold values from -11.35 to 11.35
- decay: float32 [4096, 16], P('seq'), may hold values from 0.00048828125 to 0.04
- passthrough: float32 [4096], P('seq'), may hold values from -4 to 4
Outputs:
- gated: bfloat16 [16, 2048, 4096], P('fsdp', 'seq')
The draws below stay inside these ranges and needn't reach their ends.
All inputs are finite; a program needn't handle non-finite values.
Results may differ from the reference program's by a relative error of at most 0.0064.
Values may be sent and summed in bfloat16 or wider, within the bound.
A program may use at most 128 MiB of HBM per device.

```python
import jax
import jax.numpy as jnp
from jax import lax

D = 4096
MODES = 16
SEQ_LEN = 2048
SEQS = 16


def draw_decay(key, part):
    key = jax.random.fold_in(key, 7)
    center_key, ratio_key = jax.random.split(key)
    pair_count = MODES // 2
    low_end = jnp.log(1.2 / SEQ_LEN)
    high_end = jnp.log(1.0 / 30)
    placing = jax.random.uniform(center_key, (D, pair_count), jnp.float32)
    centers = jnp.exp(low_end + (high_end - low_end) * placing)
    spread = jnp.exp(0.5 * jax.random.uniform(ratio_key, (D, pair_count), jnp.float32, jnp.log(1.2), jnp.log(1.4)))
    paired = jnp.stack([centers / spread, centers * spread], axis=-1)
    return paired.reshape(D, MODES).astype(jnp.float32)


def draw_residue(key, part):
    key = jax.random.fold_in(key, 11)
    size_key, match_key = jax.random.split(key)
    pair_count = MODES // 2
    scale_mode = 14.0 / MODES ** 0.5
    strength = jax.random.truncated_normal(size_key, -3.0, 3.0, (D, pair_count), jnp.float32)
    mismatch = jax.random.uniform(match_key, (D, pair_count), jnp.float32, 0.92, 1.08)
    paired = jnp.stack([strength, -strength * mismatch], axis=-1) * scale_mode
    return paired.reshape(D, MODES).astype(jnp.float32)


def block_levels(stream_key, shape, cuts, low, top_value):
    gain, own = 1.0, jax.random.fold_in(stream_key, 6)
    for position, blocks in cuts:
        draws = jnp.exp(jax.random.uniform(jax.random.fold_in(own, position), (blocks,), jnp.float32, low / len(cuts), top_value / len(cuts)))
        gain = gain * jnp.repeat(draws, shape[position] // blocks).reshape([-1 if axis == position else 1 for axis in range(len(shape))])
    return gain


def scatter_about(rng, extent, scale, bound, cuts=(), dtype=jnp.bfloat16):
    drawn = scale * jax.random.normal(rng, extent, jnp.float32)
    if cuts:
        drawn = drawn * block_levels(rng, extent, cuts, -0.22, 0.18)
    return jnp.clip(drawn, -bound, bound).astype(dtype)


def setup_inputs(seed: int = 0) -> dict:
    streams_of = jax.random.split(jax.random.key(seed), 9)
    return {
        "tokens": scatter_about(streams_of[0], (SEQS, SEQ_LEN, D), 1.0, 6.0, ((0, 16), (1, 16))),
        "w_query": scatter_about(streams_of[1], (D, D), D ** -0.5, 0.09375, ((0, 16), (1, 16)), jnp.float32),
        "w_key": scatter_about(streams_of[2], (D, D), D ** -0.5, 0.09375, ((0, 16), (1, 16)), jnp.float32),
        "w_value": scatter_about(streams_of[3], (D, D), D ** -0.5, 0.09375, ((0, 16), (1, 16)), jnp.float32),
        "short_taps": scatter_about(streams_of[4], (3, 3, D), 0.6, 4.0, ((2, 16),), jnp.float32),
        "residue": draw_residue(jax.random.fold_in(streams_of[8], 71), 0),
        "decay": draw_decay(jax.random.fold_in(streams_of[8], 71), 0),
        "passthrough": scatter_about(streams_of[7], (D,), 1.0, 4.0, ((0, 16),), jnp.float32),
    }


def reference(tokens, w_query, w_key, w_value, short_taps, residue, decay, passthrough):
    positions = jnp.arange(SEQ_LEN).astype(jnp.float32)
    mode_gain = residue * jnp.sqrt(decay)
    long_filter = jnp.zeros((SEQ_LEN, D), jnp.float32)
    for mode in range(MODES):
        long_filter = long_filter + mode_gain[:, mode][None, :] * jnp.exp(-decay[:, mode][None, :] * positions[:, None])
    filter_freq = jnp.fft.rfft(long_filter, n=2 * SEQ_LEN, axis=0)
    query_half = w_query.astype(jnp.bfloat16)
    key_half = w_key.astype(jnp.bfloat16)
    value_half = w_value.astype(jnp.bfloat16)

    def one_sequence(inputs):
        projected = jnp.stack([jnp.dot(inputs, query_half, preferred_element_type=jnp.float32), jnp.dot(inputs, key_half, preferred_element_type=jnp.float32), jnp.dot(inputs, value_half, preferred_element_type=jnp.float32)])
        padded = jnp.pad(projected, ((0, 0), (2, 0), (0, 0)))
        shorted = short_taps[0][:, None, :] * projected + short_taps[1][:, None, :] * padded[:, 1:-1] + short_taps[2][:, None, :] * padded[:, :-2]
        product = shorted[1] * shorted[2]
        spectrum = jnp.fft.rfft(product, n=2 * SEQ_LEN, axis=0) * filter_freq
        convolved = jnp.fft.irfft(spectrum, n=2 * SEQ_LEN, axis=0)[:SEQ_LEN]
        return (shorted[0] * (convolved + passthrough[None, :] * product)).astype(jnp.bfloat16)
    return lax.map(one_sequence, tokens)
```

```python
import functools
import jax, jax.numpy as jnp
from jax import lax
from jax.experimental import pallas as pl
from jax.experimental.pallas import tpu as pltpu
from jax.sharding import PartitionSpec as P

MODES = 16
PITCH = 264

def shift_rows(v, n, row):
    return jnp.where(row >= n, pltpu.roll(v, n, 0), 0.0)

def conv_half(acc, prod, res, taps, rates, gains, skip, unroll1=8, unroll2=8, chunk=None, emit=None):
    segs, span = 8, 256
    row = lax.broadcasted_iota(jnp.int32, (segs, 128), 0)
    wide = lambda v: jnp.broadcast_to(v, (segs, 128))
    fade = [wide(jnp.exp(-rates[r:r + 1])) for r in range(MODES)]
    def at(t, j):
        return acc[j, pl.ds(t, segs, stride=PITCH), :]
    def first(j):
        return shift_rows(at(span - 1, j), 1, row), shift_rows(at(span - 2, j), 1, row)
    tk = [wide(taps(i, 1)) for i in range(3)]
    tv = [wide(taps(i, 2)) for i in range(3)]
    def step1(t, c):
        k1, k2, v1, v2, hs = c
        k, v = at(t, 1), at(t, 2)
        p = (tk[0] * k + tk[1] * k1 + tk[2] * k2) * (tv[0] * v + tv[1] * v1 + tv[2] * v2)
        prod[pl.ds(pl.multiple_of(t * segs, segs), segs), :] = p
        return k, k1, v, v1, tuple(fade[r] * hs[r] + p for r in range(MODES))
    zero = jnp.zeros((segs, 128), jnp.float32)
    k1, k2 = first(1); v1, v2 = first(2)
    *_, hs = lax.fori_loop(0, span, step1, (k1, k2, v1, v2, (zero,) * MODES), unroll=unroll1)
    start = []
    for r in range(MODES):
        h = hs[r]
        for n in (1, 2, 4):
            h = h + wide(jnp.exp(-rates[r:r + 1] * float(span * n))) * shift_rows(h, n, row)
        start.append(shift_rows(h, 1, row))
    tq = [wide(taps(i, 0)) for i in range(3)]
    gain = [wide(gains[r:r + 1]) for r in range(MODES)]
    thru = wide(skip)
    def step2(t, c):
        q1, q2, hs = c
        q = at(t, 0)
        p = prod[pl.ds(pl.multiple_of(t * segs, segs), segs), :]
        hs = tuple(fade[r] * hs[r] + p for r in range(MODES))
        parts = [gain[r] * hs[r] for r in range(MODES)] + [thru * p]
        while len(parts) > 1:
            parts = [a + b for a, b in zip(parts[::2], parts[1::2])] + ([parts[-1]] if len(parts) % 2 else [])
        res[pl.ds(t, segs, stride=PITCH), :] = (tq[0] * q + tq[1] * q1 + tq[2] * q2) * parts[0]
        return q, q1, hs
    q1, q2 = first(0)
    c = (q1, q2, tuple(start))
    c = lax.fori_loop(0, span // 2, step2, c, unroll=unroll2)
    if emit: emit(0)
    c = lax.fori_loop(span // 2, span, step2, c, unroll=unroll2)
    if emit: emit(1)

def kernel(u1, u2, proj, taps, rates, residue, skip, out, prod, res, acc):
    def load(i, _):
        rows = pl.ds(pl.multiple_of(i * 256, 256), 256)
        for j in range(3):
            acc[j, pl.ds(pl.multiple_of(i * PITCH, 8), 256), :] = proj[rows, 128 * j:128 * j + 128]
        return 0
    lax.fori_loop(0, 8, load, 0)
    rt = rates[...]
    gains = residue[...] * jnp.sqrt(rt)
    conv_half(acc, prod, res, lambda i, j: taps[i, j:j + 1, :], rt, gains, skip[...], u1, u2)
    def cast(i, _):
        rows = pl.ds(pl.multiple_of(i * 256, 256), 256)
        out[rows, :] = res[pl.ds(pl.multiple_of(i * PITCH, 8), 256), :].astype(jnp.bfloat16)
        return 0
    lax.fori_loop(0, 8, cast, 0)

def conv(projected, short_taps, rates_t, residue_t, skip, u1=8, u2=8):
    return pl.pallas_call(functools.partial(kernel, u1, u2),
        grid=(2,),
        out_shape=jax.ShapeDtypeStruct((2048, 256), jnp.bfloat16),
        in_specs=[pl.BlockSpec((2048, 384), lambda h: (0, h)), pl.BlockSpec((3, 3, 128), lambda h: (0, 0, h)),
                  pl.BlockSpec((16, 128), lambda h: (0, h)), pl.BlockSpec((16, 128), lambda h: (0, h)), pl.BlockSpec((1, 128), lambda h: (0, h))],
        out_specs=pl.BlockSpec((2048, 128), lambda h: (0, h)),
        scratch_shapes=[pltpu.VMEM((2048, 128), jnp.float32), pltpu.VMEM((8 * PITCH, 128), jnp.float32)] + [pltpu.VMEM((3, 8 * PITCH, 128), jnp.float32)],
        compiler_params=pltpu.CompilerParams(vmem_limit_bytes=40 << 20),
    )(projected, short_taps, rates_t, residue_t, skip)


def body(tokens, w_query, w_key, w_value, short_taps, residue, decay, passthrough):
    masters = [w.astype(jnp.bfloat16) for w in (w_query, w_key, w_value)]
    masters = jnp.concatenate([w[:, h:h + 128] for h in (0, 128) for w in masters], axis=1)
    weights = lax.all_gather(masters, "fsdp", axis=0, tiled=True)
    inputs = lax.all_gather(tokens[0], "seq", axis=0, tiled=True)
    projected = jnp.dot(inputs, weights, preferred_element_type=jnp.float32)
    result = conv(projected, short_taps, decay.T, residue.T, passthrough[None])
    return lax.all_to_all(result, "seq", split_axis=0, concat_axis=1, tiled=True)[None]


def solution(mesh):
    return jax.shard_map(
        body,
        mesh=mesh,
        in_specs=(
            P("fsdp", "seq", None),
            P("fsdp", "seq"),
            P("fsdp", "seq"),
            P("fsdp", "seq"),
            P(None, None, "seq"),
            P("seq", None),
            P("seq", None),
            P("seq"),
        ),
        out_specs=P("fsdp", "seq", None),
        check_vma=False,
    )
```

```python
import functools

import jax
import jax.numpy as jnp
from jax import lax
from jax.experimental import pallas as pl
from jax.experimental.pallas import tpu as pltpu
from jax.sharding import PartitionSpec as P

MESH = pl.DeviceIdType.MESH
MODES = 16
SEGS, SPAN = 8, 256
PITCH = 264
SPLIT = 9 * 256
HALVES = (0, 1)

UP = [("o", 0, 0), ("o", 0, 1), ("o", 1, 0), ("p", 0, 0), ("o", 2, 0), ("p", 1, 0), ("o", 3, 0), ("p", 2, 0),
      ("o", 1, 1), ("p", 0, 1), ("o", 2, 1), ("p", 1, 1), ("o", 3, 1), ("p", 2, 1)]
DOWN = [("o", 0, 0), ("o", 0, 1), ("p", 0, 0), ("o", 1, 0), ("p", 1, 0), ("o", 2, 0), ("p", 2, 0), ("p", 0, 1),
        ("p", 3, 0), ("p", 1, 1), ("o", 1, 1), ("p", 2, 1), ("o", 2, 1), ("p", 3, 1)]

PIECES = {
    "AX": ("A", 1, 0, None), "AU": ("A", 0, 1, None), "AD": ("A", 0, 3, None), "AXU": ("A", 1, 1, None), "AXD": ("A", 1, 3, None),
    "AO0": ("A", 0, 2, 0), "AO1": ("A", 0, 2, 1), "AXO0": ("A", 1, 2, 0), "AXO1": ("A", 1, 2, 1),
    "BX": ("B", 1, 0, None), "BU": ("B", 0, 1, None), "BD": ("B", 0, 3, None), "BXU": ("B", 1, 1, None), "BXD": ("B", 1, 3, None),
    "BO0": ("B", 0, 2, 0), "BO1": ("B", 0, 2, 1), "BXO0": ("B", 1, 2, 0), "BXO1": ("B", 1, 2, 1),
}
NAMES = list(PIECES)


def shift_rows(v, n, row):
    return jnp.where(row >= n, pltpu.roll(v, n, 0), 0.0)


def conv_half(half, acc, prod, res, taps, rates, gains, skip, emit):
    row = lax.broadcasted_iota(jnp.int32, (SEGS, 128), 0)
    wide = lambda v: jnp.broadcast_to(v, (SEGS, 128))
    fade = [wide(jnp.exp(-rates[r:r + 1])) for r in range(MODES)]

    def at(t, j):
        return acc[3 * half + j, pl.ds(t, SEGS, stride=PITCH), :]

    def before(j):
        return shift_rows(at(SPAN - 1, j), 1, row), shift_rows(at(SPAN - 2, j), 1, row)

    tap = [[wide(taps[i, j:j + 1, half * 128:half * 128 + 128]) for i in range(3)] for j in range(3)]

    def first(t, carry):
        k1, k2, v1, v2, hs = carry
        k, v = at(t, 1), at(t, 2)
        p = (tap[1][0] * k + tap[1][1] * k1 + tap[1][2] * k2) * (tap[2][0] * v + tap[2][1] * v1 + tap[2][2] * v2)
        prod[pl.ds(pl.multiple_of(t * SEGS, SEGS), SEGS), :] = p
        return k, k1, v, v1, tuple(fade[r] * hs[r] + p for r in range(MODES))

    zero = jnp.zeros((SEGS, 128), jnp.float32)
    *_, hs = lax.fori_loop(0, SPAN, first, (*before(1), *before(2), (zero,) * MODES), unroll=8)
    start = []
    for r in range(MODES):
        h = hs[r]
        for n in (1, 2, 4):
            h = h + wide(jnp.exp(-rates[r:r + 1] * float(SPAN * n))) * shift_rows(h, n, row)
        start.append(shift_rows(h, 1, row))
    gain = [wide(gains[r:r + 1]) for r in range(MODES)]
    thru = wide(skip)

    def second(t, carry):
        q1, q2, hs = carry
        q = at(t, 0)
        p = prod[pl.ds(pl.multiple_of(t * SEGS, SEGS), SEGS), :]
        hs = tuple(fade[r] * hs[r] + p for r in range(MODES))
        parts = [gain[r] * hs[r] for r in range(MODES)] + [thru * p]
        while len(parts) > 1:
            parts = [a + b for a, b in zip(parts[::2], parts[1::2])] + ([parts[-1]] if len(parts) % 2 else [])
        res[pl.ds(t, SEGS, stride=PITCH), :] = (tap[0][0] * q + tap[0][1] * q1 + tap[0][2] * q2) * parts[0]
        return q, q1, hs

    carry = (*before(0), tuple(start))
    for core in range(2):
        carry = lax.fori_loop(core * (SPAN // 2), (core + 1) * (SPAN // 2), second, carry, unroll=8)
        emit(core)


def kernel(tokens, w_query, w_key, w_value, taps, residue, decay, skip, out,
           tok, wts, masters, acc, prod, res, stage,
           load_sem, z_send, z_recv, h_send, h_recv, t_send, t_recv, d_send, d_recv, o_send, o_recv, o_local):
    s, f = lax.axis_index("seq"), lax.axis_index("fsdp")
    xl, y, c = s // 8, (s // 2) % 4, s % 2
    xh, z = f // 8, f % 8

    def seg(dx, dy):
        return ((xl + dx) % 2) * 4 + (y + dy) % 4

    def dev(dx, dy, core):
        return (seg(dx, dy) * 2 + core, f)

    def nth(n):
        return n // 4, n % 4

    z_dev = [(s, xh * 8 + (z + 1) % 8), (s, xh * 8 + (z + 7) % 8)]
    h_dev = (s, (1 - xh) * 8 + z)
    sib = dev(0, 0, 1 - c)
    sends = []

    barrier = pltpu.get_barrier_semaphore()

    def greet(n, _):
        for core in range(2):
            pl.semaphore_signal(barrier, inc=1, device_id=dev(*nth(n), core), device_id_type=MESH)
        return 0

    lax.fori_loop(1, 8, greet, 0)
    for d in (*z_dev, h_dev, sib):
        pl.semaphore_signal(barrier, inc=1, device_id=d, device_id_type=MESH)

    def own_rows(core, half=None):
        start = (seg(0, 0) * 2 + core) * 128
        return pl.ds(pl.multiple_of(start, 128), 128)

    loads = [pltpu.make_async_copy(w, masters.at[j], load_sem.at[j]) for j, w in enumerate((w_query, w_key, w_value))]
    loads.append(pltpu.make_async_copy(tokens.at[0], tok.at[own_rows(c), :], load_sem.at[3]))
    for load in loads:
        load.start()
    for load in loads[:3]:
        load.wait()
    mine = pl.ds(pl.multiple_of(f * 256, 256), 256)
    for h in HALVES:
        for j in range(3):
            wts[h, mine, 128 * j:128 * j + 128] = masters[j, :, 128 * h:128 * h + 128].astype(jnp.bfloat16)
    rates = decay[...].T
    gains = residue[...].T * jnp.sqrt(rates)
    loads[3].wait()
    pl.semaphore_wait(barrier, 18)

    def t_ref(part, dx, dy, rows, core):
        start = (seg(dx, dy) * 2 + core) * 128 + (0 if rows is None else 64 * rows)
        rows = pl.ds(pl.multiple_of(start, 64), 128 if rows is None else 64)
        return tok.at[rows, pl.ds(0, SPLIT) if part == "A" else pl.ds(SPLIT, 4096 - SPLIT)]

    def remote(src, dst, send, recv, device):
        return pltpu.make_async_remote_copy(src_ref=src, dst_ref=dst, send_sem=send, recv_sem=recv, device_id=device, device_id_type=MESH)

    def push(part, dx, dy, rows, device, name):
        ref, n = t_ref(part, dx, dy, rows, c), NAMES.index(name)
        copy = remote(ref, ref, t_send.at[n], t_recv.at[n], device)
        copy.start()
        sends.append(copy)

    def share(n, ref):
        copy = remote(ref, ref, d_send.at[n], d_recv.at[n], sib)
        copy.start()
        sends.append(copy)

    here, shared = set(), set()

    def arrive(*names):
        for name in names:
            n, ref = NAMES.index(name), t_ref(*PIECES[name], c)
            remote(ref, ref, t_send.at[n], t_recv.at[n], sib).wait_recv()
            share(n, ref)
            here.add(name)

    def other(*names):
        for name in names:
            n, ref = NAMES.index(name), t_ref(*PIECES[name], 1 - c)
            remote(ref, ref, d_send.at[n], d_recv.at[n], sib).wait_recv()
            shared.add(name)

    up, down, across = dev(0, 1, c), dev(0, 3, c), dev(1, 0, c)
    push("A", 0, 0, None, across, "AX")
    push("B", 0, 0, None, up, "BD")
    push("B", 0, 0, None, down, "BU")

    def w_ref(h, kind, steps):
        block = (xh if kind == "o" else 1 - xh) * 8 + (z + steps) % 8
        return wts.at[h, pl.ds(pl.multiple_of(block * 256, 256), 256), :]

    hop = [remote(w_ref(h, "o", 0), w_ref(h, "o", 0), h_send.at[h], h_recv.at[h], h_dev) for h in HALVES]
    sends.extend(hop)
    arrived = {("o", 0, 0), ("o", 0, 1)}

    def place(way, kind, far):
        return 8 - far if way == 0 else far

    def w_arrive(way, kind, far, h):
        key = (kind, far if way else -far, h)
        if key in arrived:
            return
        if far == 0:
            ref = w_ref(h, "p", 0)
            remote(ref, ref, h_send.at[h], h_recv.at[h], h_dev).wait_recv()
        else:
            n = (UP, DOWN)[way].index((kind, far - 1, h))
            ref = w_ref(h, kind, place(way, kind, far))
            remote(ref, ref, z_send.at[way, n], z_recv.at[way, n], z_dev[way]).wait_recv()
        arrived.add(key)

    def z_step(n):
        for way in range(2):
            kind, far, h = (UP, DOWN)[way][n]
            w_arrive(way, kind, far, h)
            ref = w_ref(h, kind, place(way, kind, far))
            copy = remote(ref, ref, z_send.at[way, n], z_recv.at[way, n], z_dev[way])
            copy.start()
            sends.append(copy)

    hop[0].start()
    z_step(0)
    push("A", 0, 0, None, up, "AD")
    push("A", 0, 0, None, down, "AU")
    push("B", 0, 0, None, across, "BX")
    z_step(1)
    hop[1].start()
    own = tok.at[own_rows(c), :]
    share(len(NAMES), own)

    def rows_of(g):
        return pl.ds(pl.multiple_of(g * SPAN, SPAN), SPAN), pl.ds(pl.multiple_of(g * PITCH, 8), SPAN)

    def whole(h, g):
        src, dst = rows_of(g)
        r = jnp.dot(tok[src, :], wts[h], preferred_element_type=jnp.float32)
        for j in range(3):
            acc[3 * h + j, dst, :] = r[:, 128 * j:128 * j + 128]

    def some(h, g, blocks, fresh):
        src, dst = rows_of(g)
        r = None
        for kind, steps in blocks:
            block = (xh if kind == "o" else 1 - xh) * 8 + (z + steps) % 8
            at = pl.ds(pl.multiple_of(block * 256, 256), 256)
            d = jnp.dot(tok[src, at], wts[h, at, :], preferred_element_type=jnp.float32)
            r = d if r is None else r + d
        for j in range(3):
            part = r[:, 128 * j:128 * j + 128]
            acc[3 * h + j, dst, :] = part if fresh else acc[3 * h + j, dst, :] + part

    def over(order, work):
        count, place_of = order
        def one(i, _):
            work(seg(*place_of(i)))
            return 0
        lax.fori_loop(0, count, one, 0)

    near = (4, lambda i: (i // 3, i % 3 + (i % 3) // 2))
    near_a = (2, lambda i: (0, i))
    near_b = (2, lambda i: (i, 3 - 3 * i))
    side = (2, lambda i: (1, 1 + 2 * i))
    far_a = (1, lambda i: (0, 2))
    far_b = (1, lambda i: (1, 2))
    seven = (7, lambda i: ((i + 1) // 4 - (i + 1) // 8, (i + 1) % 4 - (i // 6) * 3))
    every = (8, lambda i: (i // 4, i % 4))
    groups = [
        [("o", 0), ("p", 0), ("o", 7), ("o", 1)],
        [("o", 6), ("p", 1), ("p", 7), ("p", 2)],
        [("o", 5), ("o", 2), ("p", 6), ("p", 3)],
        [("o", 4), ("o", 3), ("p", 5), ("p", 4)],
    ]
    firsts = (6, lambda i: (i // 3, i % 3 + (i % 3) // 2))
    ways = {("o", 7): (0, 1), ("o", 6): (0, 2), ("o", 5): (0, 3), ("o", 4): (0, 4), ("p", 7): (0, 1), ("p", 6): (0, 2), ("p", 5): (0, 3),
            ("o", 1): (1, 1), ("o", 2): (1, 2), ("o", 3): (1, 3), ("p", 1): (1, 1), ("p", 2): (1, 2), ("p", 3): (1, 3), ("p", 4): (1, 4),
            ("p", 0): (0, 0)}

    def have(h, blocks):
        for kind, steps in blocks:
            if (kind, steps) != ("o", 0):
                way, far = ways[kind, steps]
                w_arrive(way, kind, far, h)

    z_step(2)
    z_step(3)
    z_step(4)
    z_step(5)
    arrive("BU", "BD")
    push("B", 0, 1, None, across, "BXU")
    push("B", 0, 3, 0, up, "BO0")
    push("B", 0, 1, 1, down, "BO1")
    push("B", 0, 3, None, across, "BXD")
    arrive("AX")
    push("A", 1, 0, None, up, "AXD")
    push("A", 1, 0, None, down, "AXU")
    arrive("AU", "AD")
    push("A", 0, 3, 0, up, "AO0")
    push("A", 0, 1, 1, down, "AO1")
    arrive("BX")
    z_step(6)
    remote(own, own, d_send.at[len(NAMES)], d_recv.at[len(NAMES)], sib).wait_recv()
    other("BU", "BD", "AX", "AU", "AD", "BX")
    have(1, groups[0])
    over(near, lambda g: some(1, g, groups[0], True))
    arrive("BO0", "BO1")
    push("B", 0, 2, 0, across, "BXO0")
    push("B", 0, 2, 1, across, "BXO1")
    z_step(7)
    z_step(8)
    z_step(9)
    have(0, [key for group in groups for key in group])
    over(near_a, lambda g: whole(0, g))
    arrive("AXU", "AXD")
    push("A", 1, 3, 0, up, "AXO0")
    push("A", 1, 1, 1, down, "AXO1")
    z_step(10)
    over(near_b, lambda g: whole(0, g))
    arrive("BXU", "BXD")
    other("AXU", "AXD", "BXU", "BXD")
    over(side, lambda g: whole(0, g))
    z_step(11)
    have(1, groups[1])
    over(side, lambda g: some(1, g, groups[0] + groups[1], True))
    over(near, lambda g: some(1, g, groups[1], False))
    arrive("AO0", "AO1")
    other("BO0", "BO1", "AO0", "AO1")
    over(far_a, lambda g: whole(0, g))
    z_step(12)
    z_step(13)
    have(1, groups[2])
    over(far_a, lambda g: some(1, g, groups[0] + groups[1] + groups[2], True))
    over(firsts, lambda g: some(1, g, groups[2], False))
    arrive("BXO0", "BXO1", "AXO0", "AXO1")
    other("BXO0", "BXO1", "AXO0", "AXO1")
    over(far_b, lambda g: whole(0, g))
    over(far_b, lambda g: some(1, g, groups[0] + groups[1] + groups[2], True))

    def channels(h):
        return pl.ds(pl.multiple_of(s * 256 + h * 128, 128), 128)

    def block_copy(h, n, core):
        dx, dy = nth(n)
        block = pl.ds(pl.multiple_of((seg(dx, dy) * 2 + core) * 128, 128), 128)
        return remote(stage.at[h, block, :], out.at[0, :, channels(h)], o_send.at[h, n, core], o_recv.at[h, n, c], dev(dx, dy, core))

    def to_sibling(h):
        block = own_rows(1 - c)
        return remote(stage.at[h, block, :], out.at[0, :, channels(h)], o_send.at[h, 0, 0], o_recv.at[h, 0, 0], sib)

    def to_self(h):
        return pltpu.make_async_copy(stage.at[h, own_rows(c), :], out.at[0, :, channels(h)], o_local.at[h])

    def emit(h, core):
        def cast(g, _):
            src = pl.ds(pl.multiple_of(g * PITCH + core * 128, 8), 128)
            dst = pl.ds(pl.multiple_of(g * SPAN + core * 128, 128), 128)
            stage[h, dst, :] = res[src, :].astype(jnp.bfloat16)
            return 0
        lax.fori_loop(0, SEGS, cast, 0)
        def go(n, _):
            block_copy(h, n, core).start()
            return 0
        lax.fori_loop(1, 8, go, 0)
        if core:
            to_sibling(h).start()
            to_self(h).start()

    for h in HALVES:
        if h:
            have(1, groups[3])
            over(every, lambda g: some(1, g, groups[3], False))
        lanes = slice(h * 128, h * 128 + 128)
        conv_half(h, acc, prod, res, taps, rates[:, lanes], gains[:, lanes], skip[:, lanes], functools.partial(emit, h))

    for h in HALVES:
        def finish(n, _):
            for core in range(2):
                block_copy(h, n, core).wait_send()
                ref = out.at[0, :, channels(h)]
                remote(ref, ref, o_send.at[h, n, core], o_recv.at[h, n, core], sib).wait_recv()
            return 0
        lax.fori_loop(1, 8, finish, 0)
        to_sibling(h).wait()
        to_self(h).wait()
    for copy in sends:
        copy.wait_send()


def body(tokens, w_query, w_key, w_value, short_taps, residue, decay, passthrough):
    vmem, anywhere = pl.BlockSpec(memory_space=pltpu.VMEM), pl.BlockSpec(memory_space=pl.ANY)
    dma = pltpu.SemaphoreType.DMA
    return pl.pallas_call(
        kernel,
        out_shape=jax.ShapeDtypeStruct((1, 128, 4096), jnp.bfloat16),
        in_specs=[anywhere] * 4 + [vmem] * 4,
        out_specs=vmem,
        scratch_shapes=[
            pltpu.VMEM((2048, 4096), jnp.bfloat16),
            pltpu.VMEM((2, 4096, 384), jnp.bfloat16),
            pltpu.VMEM((3, 256, 256), jnp.float32),
            pltpu.VMEM((6, SEGS * PITCH, 128), jnp.float32),
            pltpu.VMEM((2048, 128), jnp.float32),
            pltpu.VMEM((SEGS * PITCH, 128), jnp.float32),
            pltpu.VMEM((2, 2048, 128), jnp.bfloat16),
            dma((4,)),
            dma((2, 14)), dma((2, 14)),
            dma((2,)), dma((2,)),
            dma((len(NAMES),)), dma((len(NAMES),)),
            dma((len(NAMES) + 1,)), dma((len(NAMES) + 1,)),
            dma((2, 8, 2)), dma((2, 8, 2)), dma((2,)),
        ],
        compiler_params=pltpu.CompilerParams(collective_id=0, has_side_effects=True, vmem_limit_bytes=50 << 20),
        cost_estimate=pl.CostEstimate(flops=2 * 2048 * 4096 * 768, bytes_accessed=4 << 20, transcendentals=0),
    )(tokens, w_query, w_key, w_value, short_taps, residue, decay, passthrough[None])


def solution(mesh):
    return jax.shard_map(
        body,
        mesh=mesh,
        in_specs=(
            P("fsdp", "seq", None),
            P("fsdp", "seq"),
            P("fsdp", "seq"),
            P("fsdp", "seq"),
            P(None, None, "seq"),
            P("seq", None),
            P("seq", None),
            P("seq"),
        ),
        out_specs=P("fsdp", "seq", None),
        check_vma=False,
    )
```

```python
import functools

import jax
import jax.numpy as jnp
from jax import lax
from jax.experimental import pallas as pl
from jax.experimental.pallas import tpu as pltpu
from jax.sharding import PartitionSpec as P

MESH = pl.DeviceIdType.MESH
MODES = 16
SEGS, SPAN = 8, 256
PITCH = 264
SPLIT = 10 * 256
HALVES = (0, 1)

UP = [("o", 0, 0), ("o", 0, 1), ("p", 0, 0), ("p", 0, 1), ("o", 1, 0), ("o", 1, 1), ("p", 1, 0), ("p", 1, 1),
      ("o", 2, 0), ("p", 2, 0), ("o", 2, 1), ("o", 3, 0), ("p", 2, 1), ("o", 3, 1)]
DOWN = [("o", 0, 0), ("o", 0, 1), ("p", 0, 0), ("p", 0, 1), ("o", 1, 0), ("p", 1, 0), ("o", 1, 1), ("p", 1, 1),
        ("p", 2, 0), ("o", 2, 0), ("p", 2, 1), ("p", 3, 0), ("o", 2, 1), ("p", 3, 1)]

PIECES = {
    "AX": ("A", 1, 0, None), "AU": ("A", 0, 1, None), "AD": ("A", 0, 3, None), "AXU": ("A", 1, 1, None), "AXD": ("A", 1, 3, None),
    "AO0": ("A", 0, 2, 0), "AO1": ("A", 0, 2, 1), "AXO0": ("A", 1, 2, 0), "AXO1": ("A", 1, 2, 1),
    "BX": ("B", 1, 0, None), "BU": ("B", 0, 1, None), "BD": ("B", 0, 3, None), "BXU": ("B", 1, 1, None), "BXD": ("B", 1, 3, None),
    "BO0": ("B", 0, 2, 0), "BO1": ("B", 0, 2, 1), "BXO0": ("B", 1, 2, 0), "BXO1": ("B", 1, 2, 1),
}
NAMES = list(PIECES)


def shift_rows(v, n, row):
    return jnp.where(row >= n, pltpu.roll(v, n, 0), 0.0)


def conv_half(half, acc, prod, res, taps, rates, gains, skip, emit):
    row = lax.broadcasted_iota(jnp.int32, (SEGS, 128), 0)
    wide = lambda v: jnp.broadcast_to(v, (SEGS, 128))
    fade = [wide(jnp.exp(-rates[r:r + 1])) for r in range(MODES)]

    def at(t, j):
        return acc[3 * half + j, pl.ds(t, SEGS, stride=PITCH), :]

    def before(j):
        return shift_rows(at(SPAN - 1, j), 1, row), shift_rows(at(SPAN - 2, j), 1, row)

    tap = [[wide(taps[i, j:j + 1, half * 128:half * 128 + 128]) for i in range(3)] for j in range(3)]

    def first(t, carry):
        k1, k2, v1, v2, hs = carry
        k, v = at(t, 1), at(t, 2)
        p = (tap[1][0] * k + tap[1][1] * k1 + tap[1][2] * k2) * (tap[2][0] * v + tap[2][1] * v1 + tap[2][2] * v2)
        prod[pl.ds(pl.multiple_of(t * SEGS, SEGS), SEGS), :] = p
        return k, k1, v, v1, tuple(fade[r] * hs[r] + p for r in range(MODES))

    zero = jnp.zeros((SEGS, 128), jnp.float32)
    *_, hs = lax.fori_loop(0, SPAN, first, (*before(1), *before(2), (zero,) * MODES), unroll=8)
    start = []
    for r in range(MODES):
        h = hs[r]
        for n in (1, 2, 4):
            h = h + wide(jnp.exp(-rates[r:r + 1] * float(SPAN * n))) * shift_rows(h, n, row)
        start.append(shift_rows(h, 1, row))
    gain = [wide(gains[r:r + 1]) for r in range(MODES)]
    thru = wide(skip)

    def second(t, carry):
        q1, q2, hs = carry
        q = at(t, 0)
        p = prod[pl.ds(pl.multiple_of(t * SEGS, SEGS), SEGS), :]
        hs = tuple(fade[r] * hs[r] + p for r in range(MODES))
        parts = [gain[r] * hs[r] for r in range(MODES)] + [thru * p]
        while len(parts) > 1:
            parts = [a + b for a, b in zip(parts[::2], parts[1::2])] + ([parts[-1]] if len(parts) % 2 else [])
        res[pl.ds(t, SEGS, stride=PITCH), :] = (tap[0][0] * q + tap[0][1] * q1 + tap[0][2] * q2) * parts[0]
        return q, q1, hs

    carry = (*before(0), tuple(start))
    for core in range(2):
        carry = lax.fori_loop(core * (SPAN // 2), (core + 1) * (SPAN // 2), second, carry, unroll=8)
        emit(core)


def kernel(tokens, w_query, w_key, w_value, taps_in, residue_in, decay_in, skip_in, out,
           taps, residue, decay, skip, tok, wts, masters, acc, prod, res, stage,
           load_sem, z_send, z_recv, h_send, h_recv, t_send, t_recv, d_send, d_recv, o_send, o_recv, o_local):
    s, f = lax.axis_index("seq"), lax.axis_index("fsdp")
    xl, y, c = s // 8, (s // 2) % 4, s % 2
    xh, z = f // 8, f % 8

    def seg(dx, dy):
        return ((xl + dx) % 2) * 4 + (y + dy) % 4

    def dev(dx, dy, core):
        return (seg(dx, dy) * 2 + core, f)

    def nth(n):
        return n // 4, n % 4

    z_dev = [(s, xh * 8 + (z + 1) % 8), (s, xh * 8 + (z + 7) % 8)]
    h_dev = (s, (1 - xh) * 8 + z)
    sib = dev(0, 0, 1 - c)
    sends = []

    barrier = pltpu.get_barrier_semaphore()

    def greet(n, _):
        for core in range(2):
            pl.semaphore_signal(barrier, inc=1, device_id=dev(*nth(n), core), device_id_type=MESH)
        return 0

    lax.fori_loop(1, 8, greet, 0)
    for d in (*z_dev, h_dev, sib):
        pl.semaphore_signal(barrier, inc=1, device_id=d, device_id_type=MESH)

    def own_rows(core, half=None):
        start = (seg(0, 0) * 2 + core) * 128
        return pl.ds(pl.multiple_of(start, 128), 128)

    loads = [pltpu.make_async_copy(w, masters.at[j], load_sem.at[j]) for j, w in enumerate((w_query, w_key, w_value))]
    loads.append(pltpu.make_async_copy(tokens.at[0], tok.at[own_rows(c), :], load_sem.at[3]))
    small = ((taps_in, taps), (residue_in, residue), (decay_in, decay), (skip_in, skip))
    loads += [pltpu.make_async_copy(src, dst, load_sem.at[4 + i]) for i, (src, dst) in enumerate(small)]
    for load in loads:
        load.start()
    for load in loads[:3]:
        load.wait()
    mine = pl.ds(pl.multiple_of(f * 256, 256), 256)
    for h in HALVES:
        for j in range(3):
            wts[h, mine, 128 * j:128 * j + 128] = masters[j, :, 128 * h:128 * h + 128].astype(jnp.bfloat16)
    pl.semaphore_wait(barrier, 18)

    def t_ref(part, dx, dy, rows, core):
        start = (seg(dx, dy) * 2 + core) * 128 + (0 if rows is None else 64 * rows)
        rows = pl.ds(pl.multiple_of(start, 64), 128 if rows is None else 64)
        return tok.at[rows, pl.ds(0, SPLIT) if part == "A" else pl.ds(SPLIT, 4096 - SPLIT)]

    def remote(src, dst, send, recv, device):
        return pltpu.make_async_remote_copy(src_ref=src, dst_ref=dst, send_sem=send, recv_sem=recv, device_id=device, device_id_type=MESH)

    def push(part, dx, dy, rows, device, name):
        ref, n = t_ref(part, dx, dy, rows, c), NAMES.index(name)
        copy = remote(ref, ref, t_send.at[n], t_recv.at[n], device)
        copy.start()
        sends.append(copy)

    def share(n, ref):
        copy = remote(ref, ref, d_send.at[n], d_recv.at[n], sib)
        copy.start()
        sends.append(copy)

    here, shared = set(), set()

    def arrive(*names):
        for name in names:
            n, ref = NAMES.index(name), t_ref(*PIECES[name], c)
            remote(ref, ref, t_send.at[n], t_recv.at[n], sib).wait_recv()
            share(n, ref)
            here.add(name)

    def other(*names):
        for name in names:
            n, ref = NAMES.index(name), t_ref(*PIECES[name], 1 - c)
            remote(ref, ref, d_send.at[n], d_recv.at[n], sib).wait_recv()
            shared.add(name)

    up, down, across = dev(0, 1, c), dev(0, 3, c), dev(1, 0, c)

    def w_ref(h, kind, steps):
        block = (xh if kind == "o" else 1 - xh) * 8 + (z + steps) % 8
        return wts.at[h, pl.ds(pl.multiple_of(block * 256, 256), 256), :]

    hop = [remote(w_ref(h, "o", 0), w_ref(h, "o", 0), h_send.at[h], h_recv.at[h], h_dev) for h in HALVES]
    sends.extend(hop)
    arrived = {("o", 0, 0), ("o", 0, 1)}

    def place(way, kind, far):
        return 8 - far if way == 0 else far

    def w_arrive(way, kind, far, h):
        key = (kind, far if way else -far, h)
        if key in arrived:
            return
        if far == 0:
            ref = w_ref(h, "p", 0)
            remote(ref, ref, h_send.at[h], h_recv.at[h], h_dev).wait_recv()
        else:
            n = (UP, DOWN)[way].index((kind, far - 1, h))
            ref = w_ref(h, kind, place(way, kind, far))
            remote(ref, ref, z_send.at[way, n], z_recv.at[way, n], z_dev[way]).wait_recv()
        arrived.add(key)

    def z_step(n):
        for way in range(2):
            kind, far, h = (UP, DOWN)[way][n]
            w_arrive(way, kind, far, h)
            ref = w_ref(h, kind, place(way, kind, far))
            copy = remote(ref, ref, z_send.at[way, n], z_recv.at[way, n], z_dev[way])
            copy.start()
            sends.append(copy)

    for copy in hop:
        copy.start()
    z_step(0)
    loads[3].wait()
    push("B", 0, 0, None, up, "BD")
    push("B", 0, 0, None, down, "BU")
    push("A", 0, 0, None, across, "AX")
    z_step(1)
    push("A", 0, 0, None, up, "AD")
    push("A", 0, 0, None, down, "AU")
    push("B", 0, 0, None, across, "BX")
    own = tok.at[own_rows(c), :]
    share(len(NAMES), own)

    def rows_of(g):
        return pl.ds(pl.multiple_of(g * SPAN, SPAN), SPAN), pl.ds(pl.multiple_of(g * PITCH, 8), SPAN)

    def whole(h, g):
        src, dst = rows_of(g)
        r = jnp.dot(tok[src, :], wts[h], preferred_element_type=jnp.float32)
        for j in range(3):
            acc[3 * h + j, dst, :] = r[:, 128 * j:128 * j + 128]

    def some(h, g, blocks, fresh):
        src, dst = rows_of(g)
        r = None
        for kind, steps in blocks:
            block = (xh if kind == "o" else 1 - xh) * 8 + (z + steps) % 8
            at = pl.ds(pl.multiple_of(block * 256, 256), 256)
            d = jnp.dot(tok[src, at], wts[h, at, :], preferred_element_type=jnp.float32)
            r = d if r is None else r + d
        for j in range(3):
            part = r[:, 128 * j:128 * j + 128]
            acc[3 * h + j, dst, :] = part if fresh else acc[3 * h + j, dst, :] + part

    def over(order, work):
        count, place_of = order
        def one(i, _):
            work(seg(*place_of(i)))
            return 0
        lax.fori_loop(0, count, one, 0)

    near = (3, lambda i: (0, i + i // 2))
    beside = (1, lambda i: (1, 0))
    side_up = (1, lambda i: (1, 1))
    side_down = (1, lambda i: (1, 3))
    opposite = (1, lambda i: (0, 2))
    last = (1, lambda i: (1, 2))
    every = (8, lambda i: (i // 4, i % 4))
    groups = [
        [("o", 0), ("p", 0), ("o", 7), ("o", 1), ("p", 7), ("p", 1)],
        [("o", 6), ("o", 2), ("p", 6), ("p", 2)],
        [("o", 5), ("o", 3), ("p", 5), ("p", 3)],
        [("o", 4), ("p", 4)],
    ]
    late = [("o", 3), ("p", 5), ("o", 4), ("p", 4)]
    firsts = (4, lambda i: (i // 3, i % 3 + (i % 3) // 2))
    ways = {("o", 7): (0, 1), ("o", 6): (0, 2), ("o", 5): (0, 3), ("o", 4): (0, 4), ("p", 7): (0, 1), ("p", 6): (0, 2), ("p", 5): (0, 3),
            ("o", 1): (1, 1), ("o", 2): (1, 2), ("o", 3): (1, 3), ("p", 1): (1, 1), ("p", 2): (1, 2), ("p", 3): (1, 3), ("p", 4): (1, 4),
            ("p", 0): (0, 0)}

    def have(h, blocks):
        for kind, steps in blocks:
            if (kind, steps) != ("o", 0):
                way, far = ways[kind, steps]
                w_arrive(way, kind, far, h)

    z_step(2)
    arrive("BU", "BD")
    push("B", 0, 3, 0, up, "BO0")
    push("B", 0, 1, 1, down, "BO1")
    push("B", 0, 1, None, across, "BXU")
    push("B", 0, 3, None, across, "BXD")
    z_step(3)
    z_step(4)
    z_step(5)
    z_step(6)
    z_step(7)
    arrive("AX")
    push("A", 1, 0, None, up, "AXD")
    push("A", 1, 0, None, down, "AXU")
    arrive("AU", "AD")
    push("A", 0, 3, 0, up, "AO0")
    push("A", 0, 1, 1, down, "AO1")
    z_step(8)
    remote(own, own, d_send.at[len(NAMES)], d_recv.at[len(NAMES)], sib).wait_recv()
    other("BU", "BD", "AU", "AD", "AX")
    have(0, groups[0])
    have(1, groups[0])
    over(near, lambda g: some(0, g, groups[0], True))
    arrive("BO0", "BO1")
    push("B", 0, 2, 0, across, "BXO0")
    push("B", 0, 2, 1, across, "BXO1")
    over(near, lambda g: some(1, g, groups[0], True))
    z_step(9)
    arrive("BX")
    other("BX", "BO0", "BO1")
    over(beside, lambda g: some(0, g, groups[0], True))
    over(beside, lambda g: some(1, g, groups[0], True))
    z_step(10)
    have(0, groups[1])
    have(1, groups[1])
    over(firsts, lambda g: some(0, g, groups[1], False))
    z_step(11)
    over(firsts, lambda g: some(1, g, groups[1], False))
    arrive("BXU", "AXU", "AXD")
    push("A", 1, 3, 0, up, "AXO0")
    push("A", 1, 1, 1, down, "AXO1")
    z_step(12)
    other("BXU", "AXU", "AXD")
    have(0, groups[2])
    first_ten = groups[0] + groups[1]
    over(side_up, lambda g: some(0, g, first_ten + groups[2], True))
    over(side_up, lambda g: some(1, g, first_ten, True))
    over(firsts, lambda g: some(0, g, groups[2], False))
    z_step(13)
    arrive("AO0", "AO1", "BXD")
    other("AO0", "AO1", "BXD")
    early = [("o", 5), ("p", 3)]
    have(1, early)
    over(firsts, lambda g: some(1, g, early, False))
    over(side_up, lambda g: some(1, g, early, False))
    have(0, groups[3])
    over(side_down, lambda g: whole(0, g))
    over(opposite, lambda g: whole(0, g))
    over(firsts, lambda g: some(0, g, groups[3], False))
    over(side_up, lambda g: some(0, g, groups[3], False))
    arrive("BXO0", "BXO1", "AXO0", "AXO1")
    over(side_down, lambda g: some(1, g, first_ten + early, True))
    over(opposite, lambda g: some(1, g, first_ten + early, True))
    other("BXO0", "BXO1", "AXO0", "AXO1")
    over(last, lambda g: whole(0, g))

    def channels(h):
        return pl.ds(pl.multiple_of(s * 256 + h * 128, 128), 128)

    def block_copy(h, n, core):
        dx, dy = nth(n)
        block = pl.ds(pl.multiple_of((seg(dx, dy) * 2 + core) * 128, 128), 128)
        return remote(stage.at[h, block, :], out.at[0, :, channels(h)], o_send.at[h, n, core], o_recv.at[h, n, c], dev(dx, dy, core))

    def to_sibling(h):
        block = own_rows(1 - c)
        return remote(stage.at[h, block, :], out.at[0, :, channels(h)], o_send.at[h, 0, 0], o_recv.at[h, 0, 0], sib)

    def to_self(h):
        return pltpu.make_async_copy(stage.at[h, own_rows(c), :], out.at[0, :, channels(h)], o_local.at[h])

    for load in loads[4:]:
        load.wait()
    rates = decay[...]
    gains = residue[...] * jnp.sqrt(rates)

    def emit(h, core):
        def cast(g, _):
            src = pl.ds(pl.multiple_of(g * PITCH + core * 128, 8), 128)
            dst = pl.ds(pl.multiple_of(g * SPAN + core * 128, 128), 128)
            stage[h, dst, :] = res[src, :].astype(jnp.bfloat16)
            return 0
        lax.fori_loop(0, SEGS, cast, 0)
        def go(n, _):
            block_copy(h, n, core).start()
            return 0
        lax.fori_loop(1, 8, go, 0)
        if core:
            to_sibling(h).start()
            to_self(h).start()

    for h in HALVES:
        if h:
            over(last, lambda g: some(1, g, first_ten + early, True))
            have(1, late)
            over(every, lambda g: some(1, g, late, False))
        lanes = slice(h * 128, h * 128 + 128)
        conv_half(h, acc, prod, res, taps, rates[:, lanes], gains[:, lanes], skip[0:1, lanes], functools.partial(emit, h))

    for h in HALVES:
        def finish(n, _):
            for core in range(2):
                block_copy(h, n, core).wait_send()
                ref = out.at[0, :, channels(h)]
                remote(ref, ref, o_send.at[h, n, core], o_recv.at[h, n, core], sib).wait_recv()
            return 0
        lax.fori_loop(1, 8, finish, 0)
        to_sibling(h).wait()
        to_self(h).wait()
    for copy in sends:
        copy.wait_send()


def body(tokens, w_query, w_key, w_value, short_taps, residue, decay, passthrough):
    hbm = pl.BlockSpec(memory_space=pltpu.HBM)
    dma = pltpu.SemaphoreType.DMA
    return pl.pallas_call(
        kernel,
        out_shape=jax.ShapeDtypeStruct((1, 128, 4096), jnp.bfloat16),
        in_specs=[hbm] * 8,
        out_specs=hbm,
        scratch_shapes=[
            pltpu.VMEM((3, 3, 256), jnp.float32),
            pltpu.VMEM((MODES, 256), jnp.float32),
            pltpu.VMEM((MODES, 256), jnp.float32),
            pltpu.VMEM((1, 256), jnp.float32),
            pltpu.VMEM((2048, 4096), jnp.bfloat16),
            pltpu.VMEM((2, 4096, 384), jnp.bfloat16),
            pltpu.VMEM((3, 256, 256), jnp.float32),
            pltpu.VMEM((6, SEGS * PITCH, 128), jnp.float32),
            pltpu.VMEM((2048, 128), jnp.float32),
            pltpu.VMEM((SEGS * PITCH, 128), jnp.float32),
            pltpu.VMEM((2, 2048, 128), jnp.bfloat16),
            dma((8,)),
            dma((2, 14)), dma((2, 14)),
            dma((2,)), dma((2,)),
            dma((len(NAMES),)), dma((len(NAMES),)),
            dma((len(NAMES) + 1,)), dma((len(NAMES) + 1,)),
            dma((2, 8, 2)), dma((2, 8, 2)), dma((2,)),
        ],
        compiler_params=pltpu.CompilerParams(collective_id=0, has_side_effects=True, vmem_limit_bytes=(64 << 20) - (1 << 16)),
        cost_estimate=pl.CostEstimate(flops=2 * 2048 * 4096 * 768, bytes_accessed=4 << 20, transcendentals=0),
    )(tokens, w_query, w_key, w_value, short_taps, residue.T, decay.T, passthrough[None])


def solution(mesh):
    return jax.shard_map(
        body,
        mesh=mesh,
        in_specs=(
            P("fsdp", "seq", None),
            P("fsdp", "seq"),
            P("fsdp", "seq"),
            P("fsdp", "seq"),
            P(None, None, "seq"),
            P("seq", None),
            P("seq", None),
            P("seq"),
        ),
        out_specs=P("fsdp", "seq", None),
        check_vma=False,
    )
```

```python
import functools

import jax
import jax.numpy as jnp
from jax import lax
from jax.experimental import pallas as pl
from jax.experimental.pallas import tpu as pltpu
from jax.sharding import PartitionSpec as P

MESH = pl.DeviceIdType.MESH
MODES = 16
SEGS, SPAN = 8, 256
PITCH = 264
SPLIT = 10 * 256
HALVES = (0, 1)

UP = [("o", 0, 0), ("o", 0, 1), ("p", 0, 0), ("p", 0, 1), ("o", 1, 0), ("o", 1, 1), ("p", 1, 0), ("p", 1, 1),
      ("o", 2, 0), ("p", 2, 0), ("o", 2, 1), ("o", 3, 0), ("p", 2, 1), ("o", 3, 1)]
DOWN = [("o", 0, 0), ("o", 0, 1), ("p", 0, 0), ("p", 0, 1), ("o", 1, 0), ("p", 1, 0), ("o", 1, 1), ("p", 1, 1),
        ("p", 2, 0), ("o", 2, 0), ("p", 2, 1), ("p", 3, 0), ("o", 2, 1), ("p", 3, 1)]

PIECES = {
    "AX": ("A", 1, 0, None), "AU": ("A", 0, 1, None), "AD": ("A", 0, 3, None), "AXU": ("A", 1, 1, None), "AXD": ("A", 1, 3, None),
    "AO0": ("A", 0, 2, 0), "AO1": ("A", 0, 2, 1), "AXO0": ("A", 1, 2, 0), "AXO1": ("A", 1, 2, 1),
    "BX": ("B", 1, 0, None), "BU": ("B", 0, 1, None), "BD": ("B", 0, 3, None), "BXU": ("B", 1, 1, None), "BXD": ("B", 1, 3, None),
    "BO0": ("B", 0, 2, 0), "BO1": ("B", 0, 2, 1), "BXO0": ("B", 1, 2, 0), "BXO1": ("B", 1, 2, 1),
}
NAMES = list(PIECES)


def shift_rows(v, n, row):
    return jnp.where(row >= n, pltpu.roll(v, n, 0), 0.0)


def conv_half(half, acc, prod, res, taps, rates, gains, skip, emit, ready=None, beside=None):
    row = lax.broadcasted_iota(jnp.int32, (SEGS, 128), 0)
    wide = lambda v: jnp.broadcast_to(v, (SEGS, 128))
    fade = [wide(jnp.exp(-rates[r:r + 1])) for r in range(MODES)]

    def at(t, j):
        return acc[3 * half + j, pl.ds(t, SEGS, stride=PITCH), :]

    def before(j):
        return shift_rows(at(SPAN - 1, j), 1, row), shift_rows(at(SPAN - 2, j), 1, row)

    tap = [[wide(taps[i, j:j + 1, half * 128:half * 128 + 128]) for i in range(3)] for j in range(3)]

    def first(t, carry):
        k1, k2, v1, v2, hs = carry
        k, v = at(t, 1), at(t, 2)
        p = (tap[1][0] * k + tap[1][1] * k1 + tap[1][2] * k2) * (tap[2][0] * v + tap[2][1] * v1 + tap[2][2] * v2)
        prod[pl.ds(pl.multiple_of(t * SEGS, SEGS), SEGS), :] = p
        return k, k1, v, v1, tuple(fade[r] * hs[r] + p for r in range(MODES))

    zero = jnp.zeros((SEGS, 128), jnp.float32)
    *_, hs = lax.fori_loop(0, SPAN, first, (*before(1), *before(2), (zero,) * MODES), unroll=8)
    start = []
    for r in range(MODES):
        h = hs[r]
        for n in (1, 2, 4):
            h = h + wide(jnp.exp(-rates[r:r + 1] * float(SPAN * n))) * shift_rows(h, n, row)
        start.append(shift_rows(h, 1, row))
    gain = [wide(gains[r:r + 1]) for r in range(MODES)]
    thru = wide(skip)

    def second(t, carry):
        q1, q2, hs = carry
        q = at(t, 0)
        p = prod[pl.ds(pl.multiple_of(t * SEGS, SEGS), SEGS), :]
        hs = tuple(fade[r] * hs[r] + p for r in range(MODES))
        parts = [gain[r] * hs[r] for r in range(MODES)] + [thru * p]
        while len(parts) > 1:
            parts = [a + b for a, b in zip(parts[::2], parts[1::2])] + ([parts[-1]] if len(parts) % 2 else [])
        res[pl.ds(t, SEGS, stride=PITCH), :] = (tap[0][0] * q + tap[0][1] * q1 + tap[0][2] * q2) * parts[0]
        return q, q1, hs

    def stretch(i, carry):
        beside(i)
        for u in range(SPAN // 8):
            carry = second(i * (SPAN // 8) + u, carry)
        return carry

    if ready:
        ready()
    carry = (*before(0), tuple(start))
    for core in range(2):
        if beside:
            carry = lax.fori_loop(4 * core, 4 * core + 4, stretch, carry)
        else:
            carry = lax.fori_loop(core * (SPAN // 2), (core + 1) * (SPAN // 2), second, carry, unroll=8)
        emit(core)


def kernel(tokens, w_query, w_key, w_value, taps_in, residue_in, decay_in, skip_in, out,
           taps, residue, decay, skip, tok, wts, masters, acc, prod, res, stage,
           load_sem, z_send, z_recv, h_send, h_recv, t_send, t_recv, d_send, d_recv, o_send, o_recv, o_local):
    s, f = lax.axis_index("seq"), lax.axis_index("fsdp")
    xl, y, c = s // 8, (s // 2) % 4, s % 2
    xh, z = f // 8, f % 8

    planes, rings = [xl * 4, (1 - xl) * 4], [y] + [(y + dy) % 4 for dy in (1, 2, 3)]
    chips = [[plane + ring for ring in rings] for plane in planes]

    def seg(dx, dy):
        if isinstance(dx, int) and isinstance(dy, int):
            return chips[dx % 2][dy % 4]
        return ((xl + dx) % 2) * 4 + (y + dy) % 4

    def dev(dx, dy, core):
        return (seg(dx, dy) * 2 + core, f)

    def nth(n):
        return n // 4, n % 4

    z_dev = [(s, xh * 8 + (z + 1) % 8), (s, xh * 8 + (z + 7) % 8)]
    h_dev = (s, (1 - xh) * 8 + z)
    sib = dev(0, 0, 1 - c)
    sends = []

    barrier = pltpu.get_barrier_semaphore()

    for n in range(1, 8):
        for core in range(2):
            pl.semaphore_signal(barrier, inc=1, device_id=dev(*nth(n), core), device_id_type=MESH)
    for d in (*z_dev, h_dev, sib):
        pl.semaphore_signal(barrier, inc=1, device_id=d, device_id_type=MESH)

    def own_rows(core, half=None):
        start = (seg(0, 0) * 2 + core) * 128
        return pl.ds(pl.multiple_of(start, 128), 128)

    loads = [pltpu.make_async_copy(w, masters.at[j], load_sem.at[j]) for j, w in enumerate((w_query, w_key, w_value))]
    loads.append(pltpu.make_async_copy(tokens.at[0], tok.at[own_rows(c), :], load_sem.at[3]))
    small = ((taps_in, taps), (residue_in, residue), (decay_in, decay), (skip_in, skip))
    loads += [pltpu.make_async_copy(src, dst, load_sem.at[4 + i]) for i, (src, dst) in enumerate(small)]
    for load in loads:
        load.start()
    for load in loads[:3]:
        load.wait()
    mine = pl.ds(pl.multiple_of(f * 256, 256), 256)
    for h in HALVES:
        for j in range(3):
            wts[h, mine, 128 * j:128 * j + 128] = masters[j, :, 128 * h:128 * h + 128].astype(jnp.bfloat16)
    pl.semaphore_wait(barrier, 18)

    def t_ref(part, dx, dy, rows, core):
        start = (seg(dx, dy) * 2 + core) * 128 + (0 if rows is None else 64 * rows)
        rows = pl.ds(pl.multiple_of(start, 64), 128 if rows is None else 64)
        return tok.at[rows, pl.ds(0, SPLIT) if part == "A" else pl.ds(SPLIT, 4096 - SPLIT)]

    def remote(src, dst, send, recv, device):
        return pltpu.make_async_remote_copy(src_ref=src, dst_ref=dst, send_sem=send, recv_sem=recv, device_id=device, device_id_type=MESH)

    def push(part, dx, dy, rows, device, name):
        ref, n = t_ref(part, dx, dy, rows, c), NAMES.index(name)
        copy = remote(ref, ref, t_send.at[n], t_recv.at[n], device)
        copy.start()
        sends.append(copy)

    def share(n, ref):
        copy = remote(ref, ref, d_send.at[n], d_recv.at[n], sib)
        copy.start()
        sends.append(copy)

    here, shared = set(), set()

    def arrive(*names):
        for name in names:
            n, ref = NAMES.index(name), t_ref(*PIECES[name], c)
            remote(ref, ref, t_send.at[n], t_recv.at[n], sib).wait_recv()
            share(n, ref)
            here.add(name)

    def other(*names):
        for name in names:
            n, ref = NAMES.index(name), t_ref(*PIECES[name], 1 - c)
            remote(ref, ref, d_send.at[n], d_recv.at[n], sib).wait_recv()
            shared.add(name)

    up, down, across = dev(0, 1, c), dev(0, 3, c), dev(1, 0, c)

    around = [z] + [(z + steps) % 8 for steps in range(1, 8)]
    starts = {(kind, steps): (half * 8 + around[steps]) * 256 for kind, half in (("o", xh), ("p", 1 - xh)) for steps in range(8)}

    def w_ref(h, kind, steps):
        return wts.at[h, pl.ds(pl.multiple_of(starts[kind, steps % 8], 256), 256), :]

    hop = [remote(w_ref(h, "o", 0), w_ref(h, "o", 0), h_send.at[h], h_recv.at[h], h_dev) for h in HALVES]
    sends.extend(hop)
    arrived = {("o", 0, 0), ("o", 0, 1)}

    def place(way, kind, far):
        return 8 - far if way == 0 else far

    def w_arrive(way, kind, far, h):
        key = (kind, far if way else -far, h)
        if key in arrived:
            return
        if far == 0:
            ref = w_ref(h, "p", 0)
            remote(ref, ref, h_send.at[h], h_recv.at[h], h_dev).wait_recv()
        else:
            n = (UP, DOWN)[way].index((kind, far - 1, h))
            ref = w_ref(h, kind, place(way, kind, far))
            remote(ref, ref, z_send.at[way, n], z_recv.at[way, n], z_dev[way]).wait_recv()
        arrived.add(key)

    def z_step(n):
        for way in range(2):
            kind, far, h = (UP, DOWN)[way][n]
            w_arrive(way, kind, far, h)
            ref = w_ref(h, kind, place(way, kind, far))
            copy = remote(ref, ref, z_send.at[way, n], z_recv.at[way, n], z_dev[way])
            copy.start()
            sends.append(copy)

    for copy in hop:
        copy.start()
    z_step(0)
    loads[3].wait()
    push("B", 0, 0, None, up, "BD")
    push("B", 0, 0, None, down, "BU")
    push("A", 0, 0, None, across, "AX")
    z_step(1)
    push("A", 0, 0, None, up, "AD")
    push("A", 0, 0, None, down, "AU")
    push("B", 0, 0, None, across, "BX")
    own = tok.at[own_rows(c), :]
    share(len(NAMES), own)

    def rows_of(g):
        return pl.ds(pl.multiple_of(g * SPAN, SPAN), SPAN), pl.ds(pl.multiple_of(g * PITCH, 8), SPAN)

    def whole(h, g):
        src, dst = rows_of(g)
        r = jnp.dot(tok[src, :], wts[h], preferred_element_type=jnp.float32)
        for j in range(3):
            acc[3 * h + j, dst, :] = r[:, 128 * j:128 * j + 128]

    def some(h, g, blocks, fresh):
        src, dst = rows_of(g)
        r = None
        for kind, steps in blocks:
            at = pl.ds(pl.multiple_of(starts[kind, steps], 256), 256)
            d = jnp.dot(tok[src, at], wts[h, at, :], preferred_element_type=jnp.float32)
            r = d if r is None else r + d
        for j in range(3):
            part = r[:, 128 * j:128 * j + 128]
            acc[3 * h + j, dst, :] = part if fresh else acc[3 * h + j, dst, :] + part

    def empty(g):
        for j in range(3):
            acc[3 + j, rows_of(g)[1], :] = jnp.zeros((SPAN, 128), jnp.float32)

    def over(order, work):
        count, place_of = order
        def one(i, _):
            work(seg(*place_of(i)))
            return 0
        lax.fori_loop(0, count, one, 0)

    near = (3, lambda i: (0, i + i // 2))
    beside = (1, lambda i: (1, 0))
    side_up = (1, lambda i: (1, 1))
    side_down = (1, lambda i: (1, 3))
    opposite = (1, lambda i: (0, 2))
    last = (1, lambda i: (1, 2))
    every = (8, lambda i: (i // 4, i % 4))
    groups = [
        [("o", 0), ("p", 0), ("o", 7), ("o", 1), ("p", 7), ("p", 1)],
        [("o", 6), ("o", 2), ("p", 6), ("p", 2)],
        [("o", 5), ("o", 3), ("p", 5), ("p", 3)],
        [("o", 4), ("p", 4)],
    ]
    late = [("o", 3), ("p", 5), ("o", 4), ("p", 4)]
    firsts = (4, lambda i: (i // 3, i % 3 + (i % 3) // 2))
    ways = {("o", 7): (0, 1), ("o", 6): (0, 2), ("o", 5): (0, 3), ("o", 4): (0, 4), ("p", 7): (0, 1), ("p", 6): (0, 2), ("p", 5): (0, 3),
            ("o", 1): (1, 1), ("o", 2): (1, 2), ("o", 3): (1, 3), ("p", 1): (1, 1), ("p", 2): (1, 2), ("p", 3): (1, 3), ("p", 4): (1, 4),
            ("p", 0): (0, 0)}

    def have(h, blocks):
        for kind, steps in blocks:
            if (kind, steps) != ("o", 0):
                way, far = ways[kind, steps]
                w_arrive(way, kind, far, h)

    z_step(2)
    arrive("BU", "BD")
    push("B", 0, 3, 0, up, "BO0")
    push("B", 0, 1, 1, down, "BO1")
    push("B", 0, 1, None, across, "BXU")
    push("B", 0, 3, None, across, "BXD")
    z_step(3)
    z_step(4)
    z_step(5)
    z_step(6)
    z_step(7)
    arrive("AX")
    push("A", 1, 0, None, up, "AXD")
    push("A", 1, 0, None, down, "AXU")
    arrive("AU", "AD")
    push("A", 0, 3, 0, up, "AO0")
    push("A", 0, 1, 1, down, "AO1")
    z_step(8)
    remote(own, own, d_send.at[len(NAMES)], d_recv.at[len(NAMES)], sib).wait_recv()
    other("BU", "BD", "AU", "AD", "AX")
    have(0, groups[0])
    have(1, groups[0])
    over(near, lambda g: some(0, g, groups[0], True))
    arrive("BO0", "BO1")
    push("B", 0, 2, 0, across, "BXO0")
    push("B", 0, 2, 1, across, "BXO1")
    over(near, lambda g: some(1, g, groups[0], True))
    z_step(9)
    arrive("BX")
    other("BX", "BO0", "BO1")
    over(beside, lambda g: some(0, g, groups[0], True))
    over(beside, lambda g: some(1, g, groups[0], True))
    z_step(10)
    have(0, groups[1])
    have(1, groups[1])
    over(firsts, lambda g: some(0, g, groups[1], False))
    z_step(11)
    over(firsts, lambda g: some(1, g, groups[1], False))
    arrive("BXU", "AXU", "AXD")
    push("A", 1, 3, 0, up, "AXO0")
    push("A", 1, 1, 1, down, "AXO1")
    z_step(12)
    other("BXU", "AXU", "AXD")
    have(0, groups[2])
    first_ten = groups[0] + groups[1]
    over(side_up, lambda g: some(0, g, first_ten + groups[2], True))
    over(side_up, lambda g: some(1, g, first_ten, True))
    over(firsts, lambda g: some(0, g, groups[2], False))
    z_step(13)
    arrive("AO0", "AO1", "BXD")
    other("AO0", "AO1", "BXD")
    early = [("o", 5), ("p", 3)]
    have(1, early)
    over(firsts, lambda g: some(1, g, early, False))
    over(side_up, lambda g: some(1, g, early, False))
    have(0, groups[3])
    over(side_down, lambda g: whole(0, g))
    over(opposite, lambda g: whole(0, g))
    over(firsts, lambda g: some(0, g, groups[3], False))
    over(side_up, lambda g: some(0, g, groups[3], False))
    over(last, empty)
    arrive("BXO0", "BXO1", "AXO0", "AXO1")
    over(side_down, lambda g: some(1, g, first_ten + early, True))
    over(opposite, lambda g: some(1, g, first_ten + early, True))
    other("BXO0", "BXO1", "AXO0", "AXO1")
    over(last, lambda g: whole(0, g))

    def channels(h):
        return pl.ds(pl.multiple_of(s * 256 + h * 128, 128), 128)

    def block_copy(h, n, core):
        dx, dy = nth(n)
        block = pl.ds(pl.multiple_of((seg(dx, dy) * 2 + core) * 128, 128), 128)
        return remote(stage.at[h, block, :], out.at[0, :, channels(h)], o_send.at[h, n, core], o_recv.at[h, n, c], dev(dx, dy, core))

    def to_sibling(h):
        block = own_rows(1 - c)
        return remote(stage.at[h, block, :], out.at[0, :, channels(h)], o_send.at[h, 0, 0], o_recv.at[h, 0, 0], sib)

    def to_self(h):
        return pltpu.make_async_copy(stage.at[h, own_rows(c), :], out.at[0, :, channels(h)], o_local.at[h])

    for load in loads[4:]:
        load.wait()
    rates = decay[...]
    gains = residue[...] * jnp.sqrt(rates)

    def emit(h, core):
        def cast(g, _):
            src, dst = pl.ds(g * PITCH + core * 128, 128), pl.ds(g * SPAN + core * 128, 128)
            stage[h, dst, :] = res[src, :].astype(jnp.bfloat16)
            return 0
        for g in range(SEGS):
            cast(g, 0)
        for n in range(1, 8):
            block_copy(h, n, core).start()
        if core:
            to_sibling(h).start()
            to_self(h).start()

    for h in HALVES:
        if h:
            over(last, lambda g: some(1, g, first_ten + early, False))
        lanes = slice(h * 128, h * 128 + 128)
        conv_half(h, acc, prod, res, taps, rates[:, lanes], gains[:, lanes], skip[0:1, lanes], functools.partial(emit, h),
                  *(() if h else (lambda: have(1, late), lambda g: some(1, g, late, False))))

    for h in HALVES:
        for n in range(1, 8):
            for core in range(2):
                block_copy(h, n, core).wait_send()
                ref = out.at[0, :, channels(h)]
                remote(ref, ref, o_send.at[h, n, core], o_recv.at[h, n, core], sib).wait_recv()
        to_sibling(h).wait()
        to_self(h).wait()
    for copy in sends:
        copy.wait_send()


def body(tokens, w_query, w_key, w_value, short_taps, residue, decay, passthrough):
    hbm = pl.BlockSpec(memory_space=pltpu.HBM)
    dma = pltpu.SemaphoreType.DMA
    return pl.pallas_call(
        kernel,
        out_shape=jax.ShapeDtypeStruct((1, 128, 4096), jnp.bfloat16),
        in_specs=[hbm] * 8,
        out_specs=hbm,
        scratch_shapes=[
            pltpu.VMEM((3, 3, 256), jnp.float32),
            pltpu.VMEM((MODES, 256), jnp.float32),
            pltpu.VMEM((MODES, 256), jnp.float32),
            pltpu.VMEM((1, 256), jnp.float32),
            pltpu.VMEM((2048, 4096), jnp.bfloat16),
            pltpu.VMEM((2, 4096, 384), jnp.bfloat16),
            pltpu.VMEM((3, 256, 256), jnp.float32),
            pltpu.VMEM((6, SEGS * PITCH, 128), jnp.float32),
            pltpu.VMEM((2048, 128), jnp.float32),
            pltpu.VMEM((SEGS * PITCH, 128), jnp.float32),
            pltpu.VMEM((2, 2048, 128), jnp.bfloat16),
            dma((8,)),
            dma((2, 14)), dma((2, 14)),
            dma((2,)), dma((2,)),
            dma((len(NAMES),)), dma((len(NAMES),)),
            dma((len(NAMES) + 1,)), dma((len(NAMES) + 1,)),
            dma((2, 8, 2)), dma((2, 8, 2)), dma((2,)),
        ],
        compiler_params=pltpu.CompilerParams(collective_id=0, has_side_effects=True, vmem_limit_bytes=(64 << 20) - (1 << 16)),
        cost_estimate=pl.CostEstimate(flops=2 * 2048 * 4096 * 768, bytes_accessed=4 << 20, transcendentals=0),
    )(tokens, w_query, w_key, w_value, short_taps, residue.T, decay.T, passthrough[None])


def solution(mesh):
    return jax.shard_map(
        body,
        mesh=mesh,
        in_specs=(
            P("fsdp", "seq", None),
            P("fsdp", "seq"),
            P("fsdp", "seq"),
            P("fsdp", "seq"),
            P(None, None, "seq"),
            P("seq", None),
            P("seq", None),
            P("seq"),
        ),
        out_specs=P("fsdp", "seq", None),
        check_vma=False,
    )
```

```python
import functools

import jax
import jax.numpy as jnp
from jax import lax
from jax.experimental import pallas as pl
from jax.experimental.pallas import tpu as pltpu
from jax.sharding import PartitionSpec as P

MESH = pl.DeviceIdType.MESH
MODES = 16
SEGS, SPAN = 8, 256
PITCH = 264
SPLIT = 10 * 256
HALVES = (0, 1)

UP = [("o", 0, 0), ("o", 0, 1), ("p", 0, 0), ("p", 0, 1), ("o", 1, 0), ("o", 1, 1), ("p", 1, 0), ("p", 1, 1),
      ("o", 2, 0), ("p", 2, 0), ("o", 2, 1), ("o", 3, 0), ("p", 2, 1), ("o", 3, 1)]
DOWN = [("o", 0, 0), ("o", 0, 1), ("p", 0, 0), ("p", 0, 1), ("o", 1, 0), ("p", 1, 0), ("o", 1, 1), ("p", 1, 1),
        ("p", 2, 0), ("o", 2, 0), ("p", 2, 1), ("p", 3, 0), ("o", 2, 1), ("p", 3, 1)]

PIECES = {
    "AX": ("A", 1, 0, None), "AU": ("A", 0, 1, None), "AD": ("A", 0, 3, None), "AXU": ("A", 1, 1, None), "AXD": ("A", 1, 3, None),
    "AO0": ("A", 0, 2, 0), "AO1": ("A", 0, 2, 1), "AXO0": ("A", 1, 2, 0), "AXO1": ("A", 1, 2, 1),
    "BX": ("B", 1, 0, None), "BU": ("B", 0, 1, None), "BD": ("B", 0, 3, None), "BXU": ("B", 1, 1, None), "BXD": ("B", 1, 3, None),
    "BO0": ("B", 0, 2, 0), "BO1": ("B", 0, 2, 1), "BXO0": ("B", 1, 2, 0), "BXO1": ("B", 1, 2, 1),
}
NAMES = list(PIECES)


def shift_rows(v, n, row):
    return jnp.where(row >= n, pltpu.roll(v, n, 0), 0.0)


def conv_half(half, acc, prod, res, taps, rates, gains, skip, emit, ready=None, beside=None):
    row = lax.broadcasted_iota(jnp.int32, (SEGS, 128), 0)
    wide = lambda v: jnp.broadcast_to(v, (SEGS, 128))
    fade = [wide(jnp.exp(-rates[r:r + 1])) for r in range(MODES)]

    def at(t, j):
        return acc[3 * half + j, pl.ds(t, SEGS, stride=PITCH), :]

    def before(j):
        return shift_rows(at(SPAN - 1, j), 1, row), shift_rows(at(SPAN - 2, j), 1, row)

    tap = [[wide(taps[i, j:j + 1, half * 128:half * 128 + 128]) for i in range(3)] for j in range(3)]

    def first(t, carry):
        k1, k2, v1, v2, hs = carry
        k, v = at(t, 1), at(t, 2)
        p = (tap[1][0] * k + tap[1][1] * k1 + tap[1][2] * k2) * (tap[2][0] * v + tap[2][1] * v1 + tap[2][2] * v2)
        prod[pl.ds(pl.multiple_of(t * SEGS, SEGS), SEGS), :] = p
        return k, k1, v, v1, tuple(fade[r] * hs[r] + p for r in range(MODES))

    zero = jnp.zeros((SEGS, 128), jnp.float32)
    *_, hs = lax.fori_loop(0, SPAN, first, (*before(1), *before(2), (zero,) * MODES), unroll=16)
    start = []
    for r in range(MODES):
        h = hs[r]
        for n in (1, 2, 4):
            h = h + wide(jnp.exp(-rates[r:r + 1] * float(SPAN * n))) * shift_rows(h, n, row)
        start.append(shift_rows(h, 1, row))
    gain = [wide(gains[r:r + 1]) for r in range(MODES)]
    thru = wide(skip)

    def second(t, carry):
        q1, q2, hs = carry
        q = at(t, 0)
        p = prod[pl.ds(pl.multiple_of(t * SEGS, SEGS), SEGS), :]
        hs = tuple(fade[r] * hs[r] + p for r in range(MODES))
        parts = [gain[r] * hs[r] for r in range(MODES)] + [thru * p]
        while len(parts) > 1:
            parts = [a + b for a, b in zip(parts[::2], parts[1::2])] + ([parts[-1]] if len(parts) % 2 else [])
        res[pl.ds(t, SEGS, stride=PITCH), :] = (tap[0][0] * q + tap[0][1] * q1 + tap[0][2] * q2) * parts[0]
        return q, q1, hs

    def stretch(i, carry):
        beside(i)
        for u in range(SPAN // 8):
            carry = second(i * (SPAN // 8) + u, carry)
        return carry

    if ready:
        ready()
    carry = (*before(0), tuple(start))
    for core in range(2):
        if beside:
            carry = lax.fori_loop(4 * core, 4 * core + 4, stretch, carry)
        else:
            carry = lax.fori_loop(core * (SPAN // 2), (core + 1) * (SPAN // 2), second, carry, unroll=16)
        emit(core)


def kernel(tokens, w_query, w_key, w_value, taps_in, residue_in, decay_in, skip_in, out,
           taps, residue, decay, skip, tok, wts, masters, acc, prod, res, stage,
           load_sem, z_send, z_recv, h_send, h_recv, t_send, t_recv, d_send, d_recv, o_send, o_recv, o_local):
    s, f = lax.axis_index("seq"), lax.axis_index("fsdp")
    xl, y, c = s // 8, (s // 2) % 4, s % 2
    xh, z = f // 8, f % 8

    planes, rings = [xl * 4, (1 - xl) * 4], [y] + [(y + dy) % 4 for dy in (1, 2, 3)]
    chips = [[plane + ring for ring in rings] for plane in planes]

    def seg(dx, dy):
        if isinstance(dx, int) and isinstance(dy, int):
            return chips[dx % 2][dy % 4]
        return ((xl + dx) % 2) * 4 + (y + dy) % 4

    def dev(dx, dy, core):
        return (seg(dx, dy) * 2 + core, f)

    def nth(n):
        return n // 4, n % 4

    z_dev = [(s, xh * 8 + (z + 1) % 8), (s, xh * 8 + (z + 7) % 8)]
    h_dev = (s, (1 - xh) * 8 + z)
    sib = dev(0, 0, 1 - c)
    sends = []

    barrier = pltpu.get_barrier_semaphore()

    for n in range(1, 8):
        for core in range(2):
            pl.semaphore_signal(barrier, inc=1, device_id=dev(*nth(n), core), device_id_type=MESH)
    for d in (*z_dev, h_dev, sib):
        pl.semaphore_signal(barrier, inc=1, device_id=d, device_id_type=MESH)

    def own_rows(core, half=None):
        start = (seg(0, 0) * 2 + core) * 128
        return pl.ds(pl.multiple_of(start, 128), 128)

    loads = [pltpu.make_async_copy(w, masters.at[j], load_sem.at[j]) for j, w in enumerate((w_query, w_key, w_value))]
    loads.append(pltpu.make_async_copy(tokens.at[0], tok.at[own_rows(c), :], load_sem.at[3]))
    small = ((taps_in, taps), (residue_in, residue), (decay_in, decay), (skip_in, skip))
    loads += [pltpu.make_async_copy(src, dst, load_sem.at[4 + i]) for i, (src, dst) in enumerate(small)]
    for load in loads:
        load.start()
    for load in loads[:3]:
        load.wait()
    mine = pl.ds(pl.multiple_of(f * 256, 256), 256)
    for h in HALVES:
        for j in range(3):
            wts[h, mine, 128 * j:128 * j + 128] = masters[j, :, 128 * h:128 * h + 128].astype(jnp.bfloat16)
    pl.semaphore_wait(barrier, 18)

    def t_ref(part, dx, dy, rows, core):
        start = (seg(dx, dy) * 2 + core) * 128 + (0 if rows is None else 64 * rows)
        rows = pl.ds(pl.multiple_of(start, 64), 128 if rows is None else 64)
        return tok.at[rows, pl.ds(0, SPLIT) if part == "A" else pl.ds(SPLIT, 4096 - SPLIT)]

    def remote(src, dst, send, recv, device):
        return pltpu.make_async_remote_copy(src_ref=src, dst_ref=dst, send_sem=send, recv_sem=recv, device_id=device, device_id_type=MESH)

    def push(part, dx, dy, rows, device, name):
        ref, n = t_ref(part, dx, dy, rows, c), NAMES.index(name)
        copy = remote(ref, ref, t_send.at[n], t_recv.at[n], device)
        copy.start()
        sends.append(copy)

    def share(n, ref):
        copy = remote(ref, ref, d_send.at[n], d_recv.at[n], sib)
        copy.start()
        sends.append(copy)

    here, shared = set(), set()

    def arrive(*names):
        for name in names:
            n, ref = NAMES.index(name), t_ref(*PIECES[name], c)
            remote(ref, ref, t_send.at[n], t_recv.at[n], sib).wait_recv()
            share(n, ref)
            here.add(name)

    def other(*names):
        for name in names:
            n, ref = NAMES.index(name), t_ref(*PIECES[name], 1 - c)
            remote(ref, ref, d_send.at[n], d_recv.at[n], sib).wait_recv()
            shared.add(name)

    up, down, across = dev(0, 1, c), dev(0, 3, c), dev(1, 0, c)

    around = [z] + [(z + steps) % 8 for steps in range(1, 8)]
    starts = {(kind, steps): (half * 8 + around[steps]) * 256 for kind, half in (("o", xh), ("p", 1 - xh)) for steps in range(8)}

    def w_ref(h, kind, steps):
        return wts.at[h, pl.ds(pl.multiple_of(starts[kind, steps % 8], 256), 256), :]

    hop = [remote(w_ref(h, "o", 0), w_ref(h, "o", 0), h_send.at[h], h_recv.at[h], h_dev) for h in HALVES]
    sends.extend(hop)
    arrived = {("o", 0, 0), ("o", 0, 1)}

    def place(way, kind, far):
        return 8 - far if way == 0 else far

    def w_arrive(way, kind, far, h):
        key = (kind, far if way else -far, h)
        if key in arrived:
            return
        if far == 0:
            ref = w_ref(h, "p", 0)
            remote(ref, ref, h_send.at[h], h_recv.at[h], h_dev).wait_recv()
        else:
            n = (UP, DOWN)[way].index((kind, far - 1, h))
            ref = w_ref(h, kind, place(way, kind, far))
            remote(ref, ref, z_send.at[way, n], z_recv.at[way, n], z_dev[way]).wait_recv()
        arrived.add(key)

    def z_step(n):
        for way in range(2):
            kind, far, h = (UP, DOWN)[way][n]
            w_arrive(way, kind, far, h)
            ref = w_ref(h, kind, place(way, kind, far))
            copy = remote(ref, ref, z_send.at[way, n], z_recv.at[way, n], z_dev[way])
            copy.start()
            sends.append(copy)

    for copy in hop:
        copy.start()
    z_step(0)
    loads[3].wait()
    push("B", 0, 0, None, up, "BD")
    push("B", 0, 0, None, down, "BU")
    push("A", 0, 0, None, across, "AX")
    z_step(1)
    push("A", 0, 0, None, up, "AD")
    push("A", 0, 0, None, down, "AU")
    push("B", 0, 0, None, across, "BX")
    own = tok.at[own_rows(c), :]
    share(len(NAMES), own)

    def rows_of(g):
        return pl.ds(pl.multiple_of(g * SPAN, SPAN), SPAN), pl.ds(pl.multiple_of(g * PITCH, 8), SPAN)

    def whole(h, g):
        src, dst = rows_of(g)
        r = jnp.dot(tok[src, :], wts[h], preferred_element_type=jnp.float32)
        for j in range(3):
            acc[3 * h + j, dst, :] = r[:, 128 * j:128 * j + 128]

    def some(h, g, blocks, fresh):
        src, dst = rows_of(g)
        r = None
        for kind, steps in blocks:
            at = pl.ds(pl.multiple_of(starts[kind, steps], 256), 256)
            d = jnp.dot(tok[src, at], wts[h, at, :], preferred_element_type=jnp.float32)
            r = d if r is None else r + d
        for j in range(3):
            part = r[:, 128 * j:128 * j + 128]
            acc[3 * h + j, dst, :] = part if fresh else acc[3 * h + j, dst, :] + part

    def empty(g):
        for j in range(3):
            acc[3 + j, rows_of(g)[1], :] = jnp.zeros((SPAN, 128), jnp.float32)

    def over(order, work):
        count, place_of = order
        def one(i, _):
            work(seg(*place_of(i)))
            return 0
        lax.fori_loop(0, count, one, 0)

    near = (3, lambda i: (0, i + i // 2))
    beside = (1, lambda i: (1, 0))
    side_up = (1, lambda i: (1, 1))
    side_down = (1, lambda i: (1, 3))
    opposite = (1, lambda i: (0, 2))
    last = (1, lambda i: (1, 2))
    every = (8, lambda i: (i // 4, i % 4))
    groups = [
        [("o", 0), ("p", 0), ("o", 7), ("o", 1), ("p", 7), ("p", 1)],
        [("o", 6), ("o", 2), ("p", 6), ("p", 2)],
        [("o", 5), ("o", 3), ("p", 5), ("p", 3)],
        [("o", 4), ("p", 4)],
    ]
    late = [("o", 3), ("p", 5), ("o", 4), ("p", 4)]
    firsts = (4, lambda i: (i // 3, i % 3 + (i % 3) // 2))
    ways = {("o", 7): (0, 1), ("o", 6): (0, 2), ("o", 5): (0, 3), ("o", 4): (0, 4), ("p", 7): (0, 1), ("p", 6): (0, 2), ("p", 5): (0, 3),
            ("o", 1): (1, 1), ("o", 2): (1, 2), ("o", 3): (1, 3), ("p", 1): (1, 1), ("p", 2): (1, 2), ("p", 3): (1, 3), ("p", 4): (1, 4),
            ("p", 0): (0, 0)}

    def have(h, blocks):
        for kind, steps in blocks:
            if (kind, steps) != ("o", 0):
                way, far = ways[kind, steps]
                w_arrive(way, kind, far, h)

    z_step(2)
    arrive("BU", "BD")
    push("B", 0, 3, 0, up, "BO0")
    push("B", 0, 1, 1, down, "BO1")
    push("B", 0, 1, None, across, "BXU")
    push("B", 0, 3, None, across, "BXD")
    z_step(3)
    z_step(4)
    z_step(5)
    z_step(6)
    z_step(7)
    arrive("AX")
    push("A", 1, 0, None, up, "AXD")
    push("A", 1, 0, None, down, "AXU")
    arrive("AU", "AD")
    push("A", 0, 3, 0, up, "AO0")
    push("A", 0, 1, 1, down, "AO1")
    z_step(8)
    remote(own, own, d_send.at[len(NAMES)], d_recv.at[len(NAMES)], sib).wait_recv()
    other("BU", "BD", "AU", "AD", "AX")
    have(0, groups[0])
    have(1, groups[0])
    over(near, lambda g: some(0, g, groups[0], True))
    arrive("BO0", "BO1")
    push("B", 0, 2, 0, across, "BXO0")
    push("B", 0, 2, 1, across, "BXO1")
    over(near, lambda g: some(1, g, groups[0], True))
    z_step(9)
    arrive("BX")
    other("BX", "BO0", "BO1")
    over(beside, lambda g: some(0, g, groups[0], True))
    over(beside, lambda g: some(1, g, groups[0], True))
    z_step(10)
    have(0, groups[1])
    have(1, groups[1])
    over(firsts, lambda g: some(0, g, groups[1], False))
    z_step(11)
    over(firsts, lambda g: some(1, g, groups[1], False))
    arrive("BXU", "AXU", "AXD")
    push("A", 1, 3, 0, up, "AXO0")
    push("A", 1, 1, 1, down, "AXO1")
    z_step(12)
    other("BXU", "AXU", "AXD")
    have(0, groups[2])
    first_ten = groups[0] + groups[1]
    over(side_up, lambda g: some(0, g, first_ten + groups[2], True))
    over(side_up, lambda g: some(1, g, first_ten, True))
    over(firsts, lambda g: some(0, g, groups[2], False))
    z_step(13)
    arrive("AO0", "AO1", "BXD")
    other("AO0", "AO1", "BXD")
    early = [("o", 5), ("p", 3)]
    have(1, early)
    over(firsts, lambda g: some(1, g, early, False))
    over(side_up, lambda g: some(1, g, early, False))
    have(0, groups[3])
    over(side_down, lambda g: whole(0, g))
    over(opposite, lambda g: whole(0, g))
    over(firsts, lambda g: some(0, g, groups[3], False))
    over(side_up, lambda g: some(0, g, groups[3], False))
    over(last, empty)
    arrive("BXO0", "BXO1", "AXO0", "AXO1")
    over(side_down, lambda g: some(1, g, first_ten + early, True))
    over(opposite, lambda g: some(1, g, first_ten + early, True))
    other("BXO0", "BXO1", "AXO0", "AXO1")
    over(last, lambda g: whole(0, g))

    def channels(h):
        return pl.ds(pl.multiple_of(s * 256 + h * 128, 128), 128)

    def block_copy(h, n, core):
        dx, dy = nth(n)
        block = pl.ds(pl.multiple_of((seg(dx, dy) * 2 + core) * 128, 128), 128)
        return remote(stage.at[h, block, :], out.at[0, :, channels(h)], o_send.at[h, n, core], o_recv.at[h, n, c], dev(dx, dy, core))

    def to_sibling(h):
        block = own_rows(1 - c)
        return remote(stage.at[h, block, :], out.at[0, :, channels(h)], o_send.at[h, 0, 0], o_recv.at[h, 0, 0], sib)

    def to_self(h):
        return pltpu.make_async_copy(stage.at[h, own_rows(c), :], out.at[0, :, channels(h)], o_local.at[h])

    for load in loads[4:]:
        load.wait()
    rates = decay[...]
    gains = residue[...] * jnp.sqrt(rates)

    def emit(h, core):
        def cast(g, _):
            src, dst = pl.ds(g * PITCH + core * 128, 128), pl.ds(g * SPAN + core * 128, 128)
            stage[h, dst, :] = res[src, :].astype(jnp.bfloat16)
            return 0
        for g in range(SEGS):
            cast(g, 0)
        for n in range(1, 8):
            block_copy(h, n, core).start()
        if core:
            to_sibling(h).start()
            to_self(h).start()

    for h in HALVES:
        if h:
            over(last, lambda g: some(1, g, first_ten + early, False))
        lanes = slice(h * 128, h * 128 + 128)
        conv_half(h, acc, prod, res, taps, rates[:, lanes], gains[:, lanes], skip[0:1, lanes], functools.partial(emit, h),
                  *(() if h else (lambda: have(1, late), lambda g: some(1, g, late, False))))

    for h in HALVES:
        for n in range(1, 8):
            for core in range(2):
                block_copy(h, n, core).wait_send()
                ref = out.at[0, :, channels(h)]
                remote(ref, ref, o_send.at[h, n, core], o_recv.at[h, n, core], sib).wait_recv()
        to_sibling(h).wait()
        to_self(h).wait()
    for copy in sends:
        copy.wait_send()


def body(tokens, w_query, w_key, w_value, short_taps, residue, decay, passthrough):
    hbm = pl.BlockSpec(memory_space=pltpu.HBM)
    dma = pltpu.SemaphoreType.DMA
    return pl.pallas_call(
        kernel,
        out_shape=jax.ShapeDtypeStruct((1, 128, 4096), jnp.bfloat16),
        in_specs=[hbm] * 8,
        out_specs=hbm,
        scratch_shapes=[
            pltpu.VMEM((3, 3, 256), jnp.float32),
            pltpu.VMEM((MODES, 256), jnp.float32),
            pltpu.VMEM((MODES, 256), jnp.float32),
            pltpu.VMEM((1, 256), jnp.float32),
            pltpu.VMEM((2048, 4096), jnp.bfloat16),
            pltpu.VMEM((2, 4096, 384), jnp.bfloat16),
            pltpu.VMEM((3, 256, 256), jnp.float32),
            pltpu.VMEM((6, SEGS * PITCH, 128), jnp.float32),
            pltpu.VMEM((2048, 128), jnp.float32),
            pltpu.VMEM((SEGS * PITCH, 128), jnp.float32),
            pltpu.VMEM((2, 2048, 128), jnp.bfloat16),
            dma((8,)),
            dma((2, 14)), dma((2, 14)),
            dma((2,)), dma((2,)),
            dma((len(NAMES),)), dma((len(NAMES),)),
            dma((len(NAMES) + 1,)), dma((len(NAMES) + 1,)),
            dma((2, 8, 2)), dma((2, 8, 2)), dma((2,)),
        ],
        compiler_params=pltpu.CompilerParams(collective_id=0, has_side_effects=True, vmem_limit_bytes=(64 << 20) - (1 << 16)),
        cost_estimate=pl.CostEstimate(flops=2 * 2048 * 4096 * 768, bytes_accessed=4 << 20, transcendentals=0),
    )(tokens, w_query, w_key, w_value, short_taps, residue.T, decay.T, passthrough[None])


def solution(mesh):
    return jax.shard_map(
        body,
        mesh=mesh,
        in_specs=(
            P("fsdp", "seq", None),
            P("fsdp", "seq"),
            P("fsdp", "seq"),
            P("fsdp", "seq"),
            P(None, None, "seq"),
            P("seq", None),
            P("seq", None),
            P("seq"),
        ),
        out_specs=P("fsdp", "seq", None),
        check_vma=False,
    )
```
